768 devices in a mesh: dp: 96 (over x, z_lo, y), tensor: 8 (over z_hi, core).
Axes of the slice: x: 4, y: 8, z: 12 (z_hi: 4, z_lo: 3; z = z_hi * 3 + z_lo), core: 2. Of those that a mesh axis runs over, the one named last changes fastest.
Arguments:
- decode_states: bfloat16 [12288, 12288], P('dp'), may hold values from -6 to 6
- query_weight: float32 [12288, 1024], P('dp', 'tensor'), may hold values from -0.3125 to 0.3125
- query_exponents: int32 [96, 8], P('dp', 'tensor'), may hold values from -16 to -13
- output_weight: float32 [1024, 12288], P('tensor', 'dp'), may hold values from -0.4375 to 0.4375
- output_exponents: int32 [8, 96], P('tensor', 'dp'), may hold values from -15 to -12
Outputs:
- mixed: bfloat16 [12288, 12288], P('dp', 'tensor')
The draws below stay inside these ranges and needn't reach their ends.
All inputs are finite; a program needn't handle non-finite values.
Results may differ from the reference program's by a relative error of at most 0.017.
Values may be sent and summed in bfloat16 or wider, within the bound.
A program may use at most 32 MiB of HBM per device.

```python
import jax
import jax.numpy as jnp
from jax import lax

D_WIN = 12288
HD = 128
BLK = 128
HEAD_DEV = 1
HEADS = 8
ROWS_ALL = 12288
N_TENSOR = 8


def touch_ends(array, key, least, largest):
    index_at = [jax.random.randint(jax.random.fold_in(key, axis), (), 0, length) for axis, length in enumerate(array.shape)]
    longest = array.shape.index(max(array.shape))
    neighbour = index_at[:longest] + [(index_at[longest] + 1) % array.shape[longest]] + index_at[longest + 1:]
    return array.at[tuple(index_at)].set(least).at[tuple(neighbour)].set(largest)


def level_of(key, extent, cuts, low, largest):
    def one(position, blocks):
        heights = jax.random.uniform(jax.random.fold_in(jax.random.fold_in(key, 6), position), (blocks,), jnp.float32, low / len(cuts), largest / len(cuts))
        return jnp.repeat(jnp.exp(heights), extent[position] // blocks).reshape((-1,) + (1,) * (len(extent) - position - 1))

    loudness = one(*cuts[0])
    for cut in cuts[1:]:
        loudness = loudness * one(*cut)
    return loudness


def noise(rng, dims, deviation, bound, split=(), held_as=jnp.bfloat16):
    values = jax.random.normal(rng, dims, jnp.float32) * deviation
    if len(split) > 0:
        values = level_of(rng, dims, split, -0.22, 0.18) * values
    return jnp.clip(values, min=-bound, max=bound).astype(held_as)


def setup_inputs(seed: int = 0) -> dict:
    key_list = jax.random.split(jax.random.key(seed), 6)
    decode_states = noise(key_list[0], (ROWS_ALL, D_WIN), ((12288 / D_WIN) ** 0.5 * (1024 / (HEADS * HD)) ** 0.5), 6.0, ((0, 96),))
    query_weight = noise(key_list[1], (D_WIN, HEADS * HD), 0.02, 0.3125, ((0, 96), (1, 8)), jnp.float32)
    query_exponents = touch_ends(jax.random.randint(key_list[2], (D_WIN // BLK, HEADS * HD // BLK), -16, -12), jax.random.fold_in(key_list[2], 1), -16, (-12) - 1).astype(jnp.int32)
    output_weight = noise(key_list[3], (HEADS * HD, D_WIN), 0.03, 0.4375, ((0, 8), (1, 96)), jnp.float32)
    output_exponents = touch_ends(jax.random.randint(key_list[4], (HEADS * HD // BLK, D_WIN // BLK), -15, -11), jax.random.fold_in(key_list[4], 1), -15, (-11) - 1).astype(jnp.int32)
    return dict(decode_states=decode_states, query_weight=query_weight, query_exponents=query_exponents, output_weight=output_weight, output_exponents=output_exponents)


def quantize(weight, exponents):
    power = exponents.astype(jnp.float32)
    inverse = lax.optimization_barrier(jnp.exp2(-power).astype(jnp.bfloat16)).astype(jnp.float32)
    scales = jnp.exp2(power).astype(jnp.bfloat16)
    inverse_full = jnp.repeat(jnp.repeat(inverse, BLK, axis=0), BLK, axis=1)
    scales_full = jnp.repeat(jnp.repeat(scales, BLK, axis=0), BLK, axis=1)
    codes = jnp.clip(weight * inverse_full, -448.0, 448.0).astype(jnp.bfloat16)
    return codes * scales_full


def reference(decode_states, query_weight, query_exponents, output_weight, output_exponents):
    query_dense = quantize(query_weight, query_exponents)
    output_dense = quantize(output_weight, output_exponents)
    queries = jnp.dot(decode_states, query_dense, preferred_element_type=jnp.float32).astype(jnp.bfloat16)
    group_width = HEAD_DEV * HD
    summed = jnp.zeros((decode_states.shape[0], output_dense.shape[1]), jnp.float32)
    for group in range(N_TENSOR):
        lower = group * group_width
        partial_value = jnp.dot(queries[:, lower:lower + group_width], output_dense[lower:lower + group_width, :], preferred_element_type=jnp.float32)
        partial_value = lax.optimization_barrier(partial_value.astype(jnp.bfloat16)).astype(jnp.float32)
        summed = summed + partial_value
    return summed.astype(jnp.bfloat16)
```

```python
import functools

import jax
import jax.numpy as jnp
from jax import lax
from jax.experimental import pallas as pl
from jax.experimental.pallas import tpu as pltpu
from jax.sharding import PartitionSpec as P

MESH = pl.DeviceIdType.MESH
NX, NY, NZ, NH = 4, 8, 3, 4
BLK = 128
HALF = NZ * NY // 2


def device(x, y, zl, zh, c):
    return ((x * NZ + zl) * NY + y, zh * 2 + c)


def ring_order(n):
    return jnp.where(n % 2 == 1, (n + 1) // 2, (NY - n // 2) % NY)


def dense_block(weight_ref, exponent_ref):
    power = exponent_ref[...].astype(jnp.float32)
    inverse = jnp.exp2(-power).astype(jnp.bfloat16).astype(jnp.float32)
    scale = jnp.exp2(power).astype(jnp.bfloat16).astype(jnp.float32)
    codes = jnp.clip(weight_ref[...] * inverse, -448.0, 448.0).astype(jnp.bfloat16)
    return (codes.astype(jnp.float32) * scale).astype(jnp.bfloat16)


def kernel(x_hbm, qw_ref, qe_ref, ow_ref, oe_ref, out_ref,
           xv, wq, wo, wos, qacc, qcat, acc, pout, pin,
           x_sem, wq_send, wq_recv, wo_send, wo_recv, a_send, b_send, q_send, q_recv, p_send, p_recv):
    d = lax.axis_index("dp")
    t = lax.axis_index("tensor")
    y = d % NY
    zl = (d // NY) % NZ
    x = d // (NY * NZ)
    zh = t // 2
    c = t % 2
    collector = x == zh

    def at(dx=0, dy=0, dz=0, dh=0, dc=0):
        return device((x + dx) % NX, (y + dy) % NY, (zl + dz) % NZ, (zh + dh) % NH, (c + dc) % 2)

    x_copy = pltpu.make_async_copy(x_hbm, xv, x_sem)
    x_copy.start()

    barrier = pltpu.get_barrier_semaphore()
    partners = [at(dy=k) for k in range(1, NY)] + [at(dz=k) for k in range(1, NZ)]
    partners += [at(dx=k) for k in range(1, NX)] + [at(dh=k) for k in range(1, NH)] + [at(dc=1)]
    for partner in partners:
        pl.semaphore_signal(barrier, inc=1, device_id=partner, device_id_type=MESH)

    def qi(dx, dz, dy):
        return (((x + dx) % NX) * NZ + (zl + dz) % NZ) * NY + (y + dy) % NY

    def oi(dz, dy, h):
        return (((zl + dz) % NZ) * NY + (y + dy) % NY) * NH + h

    own_q = qi(0, 0, 0)
    own_o = oi(0, 0, zh)
    wq[own_q] = dense_block(qw_ref, qe_ref)
    wos[...] = dense_block(ow_ref, oe_ref)

    @pl.when(collector)
    def _():
        wo[own_o] = wos[...]

    pl.semaphore_wait(barrier, len(partners))

    def q_copy(b, to):
        return pltpu.make_async_remote_copy(wq.at[b], wq.at[b], wq_send, wq_recv.at[b], device_id=to, device_id_type=MESH)

    def o_copy(b, to, sem):
        return pltpu.make_async_remote_copy(wo.at[b], wo.at[b], sem, wo_recv.at[b], device_id=to, device_id_type=MESH)

    def q_wait(b):
        q_copy(b, at(dx=1)).wait_recv()

    def o_wait(b):
        o_copy(b, at(dx=1), wo_send).wait_recv()

    def a_copy():
        to = device(x, y, zl, x, c)
        return pltpu.make_async_remote_copy(wos, wo.at[own_o], a_send, wo_recv.at[own_o], device_id=to, device_id_type=MESH)

    @pl.when(jnp.logical_not(collector))
    def _():
        a_copy().start()

    q_copy(own_q, at(dx=1)).start()
    q_copy(own_q, at(dx=3)).start()
    for k in (1, 7, 2, 6, 3, 5, 4):
        q_copy(own_q, at(dy=k)).start()
    for k in (1, 2):
        q_copy(own_q, at(dz=k)).start()

    @pl.loop(1, NY)
    def _(n):
        b = qi(0, 0, ring_order(n))
        q_wait(b)
        q_copy(b, at(dx=1)).start()
        q_copy(b, at(dx=3)).start()
        q_copy(b, at(dz=1)).start()
        q_copy(b, at(dz=2)).start()

    def o_spread(b):
        o_copy(b, at(dy=1), wo_send).start()
        o_copy(b, at(dy=7), wo_send).start()

    def o_first(b):
        o_spread(b)
        o_copy(b, at(dz=1), wo_send).start()
        o_copy(b, at(dz=2), wo_send).start()

    @pl.when(collector)
    def _():
        @pl.loop(0, NH)
        def _(i):
            b = oi(0, 0, (zh + i) % NH)

            @pl.when(i > 0)
            def _():
                o_wait(b)

            for k in (1, 3, 2):
                o_copy(b, at(dx=k), b_send).start()
            o_first(b)

    @pl.loop(0, NY)
    def _(n):
        for dz in (1, 2):
            b = qi(0, dz, ring_order(n))
            q_wait(b)
            q_copy(b, at(dx=1)).start()
            q_copy(b, at(dx=3)).start()

    @pl.when(jnp.logical_not(collector))
    def _():
        @pl.loop(0, NH)
        def _(i):
            b = oi(0, 0, (zh + i) % NH)
            o_wait(b)
            o_first(b)

    @pl.loop(0, NH)
    def _(i):
        for dz in (1, 2):
            b = oi(dz, 0, (zh + i) % NH)
            o_wait(b)
            o_spread(b)

    def q_forward(m):
        late = m - NY
        dz = jnp.where(m < NY, 0, 1 + late % 2)
        dy = ring_order(jnp.where(m < NY, m, late // 2))
        even = ((y + dy) % NY) % 2 == 0
        left = qi(3, dz, dy)
        right = qi(1, dz, dy)
        q_wait(left)

        @pl.when(even)
        def _():
            q_copy(left, at(dx=1)).start()

        q_wait(right)

        @pl.when(jnp.logical_not(even))
        def _():
            q_copy(right, at(dx=3)).start()

    @pl.loop(0, NZ * NY)
    def _(m):
        q_forward(m)
        k = 1 + m // 12
        r = m % 12
        h = (zh + r % NH) % NH
        left = oi(r // NH, NY - k, h)
        right = oi(r // NH, k, h)
        o_wait(left)
        o_copy(left, at(dy=1), wo_send).start()
        o_wait(right)
        o_copy(right, at(dy=7), wo_send).start()

    x_copy.wait()
    qacc[...] = jnp.zeros_like(qacc)

    def q_dot(chunk):
        columns = pl.ds(pl.multiple_of(chunk * (NY * BLK), NY * BLK), NY * BLK)
        w = wq[pl.ds(chunk * NY, NY)].reshape(NY * BLK, BLK)
        qacc[...] += jnp.dot(xv[:, columns], w, preferred_element_type=jnp.float32)

    @pl.loop(0, 12)
    def _(r):
        h = (zh + r % NH) % NH
        left = oi(r // NH, NY - 3, h)
        right = oi(r // NH, 3, h)
        o_wait(left)

        @pl.when(h < 2)
        def _():
            o_copy(left, at(dy=1), wo_send).start()

        o_wait(right)

        @pl.when(h >= 2)
        def _():
            o_copy(right, at(dy=7), wo_send).start()

        @pl.when(r < 9)
        def _():
            plane = r // 3
            dx = jnp.where(plane == 0, 0, jnp.where(plane == 1, 3, 1))
            q_dot(((x + dx) % NX) * NZ + r % NZ)

    @pl.loop(0, NZ)
    def _(dz):
        @pl.loop(0, NY)
        def _(n):
            q_wait(qi(2, dz, ring_order(n)))

        q_dot(((x + 2) % NX) * NZ + (zl + dz) % NZ)

    own_cols = qcat.at[:, pl.ds(pl.multiple_of(zh * BLK, BLK), BLK)]
    own_cols[...] = qacc[...].astype(jnp.bfloat16)

    def x_query(k):
        return pltpu.make_async_remote_copy(
            own_cols, own_cols, q_send.at[k], q_recv.at[zh], device_id=at(dh=k), device_id_type=MESH)

    for k in (2, 1, 3):
        x_query(k).start()

    @pl.loop(0, 12)
    def _(r):
        o_wait(oi(r // NH, 4, r % NH))

    for k in (1, 2, 3):
        h = (zh + k) % NH
        cols = qcat.at[:, pl.ds(pl.multiple_of(h * BLK, BLK), BLK)]
        pltpu.make_async_remote_copy(cols, cols, q_send.at[k], q_recv.at[h], device_id=at(dh=k), device_id_type=MESH).wait_recv()

    def half_sum(j):
        w = wo[pl.ds(j * NH, NH)].reshape(NH * BLK, BLK)
        return jnp.dot(qcat[...], w, preferred_element_type=jnp.float32)

    def p_copy(j):
        return pltpu.make_async_remote_copy(pout.at[j], pin.at[j], p_send.at[j], p_recv.at[j], device_id=at(dc=1), device_id_type=MESH)

    @pl.loop(0, HALF)
    def _(j):
        pout[j] = half_sum((1 - c) * HALF + j).astype(jnp.bfloat16)
        p_copy(j).start()

    @pl.loop(0, HALF)
    def _(j):
        acc[j] = half_sum(c * HALF + j)

    for j in range(HALF):
        p_copy(j).wait_recv()
        out_ref[:, j * BLK:(j + 1) * BLK] = (acc[j] + pin[j].astype(jnp.float32)).astype(jnp.bfloat16)

    for j in range(HALF):
        p_copy(j).wait_send()
    for k in (1, 2, 3):
        x_query(k).wait_send()
    sent = wq.at[pl.ds(0, 95)]
    pltpu.make_async_remote_copy(sent, sent, wq_send, wq_recv.at[0], device_id=at(dx=1), device_id_type=MESH).wait_send()
    sent = wo.at[pl.ds(0, 92)]
    pltpu.make_async_remote_copy(sent, sent, wo_send, wo_recv.at[0], device_id=at(dx=1), device_id_type=MESH).wait_send()

    @pl.when(collector)
    def _():
        some = wo.at[pl.ds(0, 12)]
        pltpu.make_async_remote_copy(some, some, b_send, wo_recv.at[0], device_id=at(dx=1), device_id_type=MESH).wait_send()

    @pl.when(jnp.logical_not(collector))
    def _():
        a_copy().wait_send()


def per_device(decode_states, query_weight, query_exponents, output_weight, output_exponents):
    rows, width = decode_states.shape
    vmem = pl.BlockSpec(memory_space=pltpu.VMEM)
    bf16, f32 = jnp.bfloat16, jnp.float32
    dma = pltpu.SemaphoreType.DMA
    return pl.pallas_call(
        kernel,
        out_shape=jax.ShapeDtypeStruct((rows, HALF * BLK), bf16),
        in_specs=[pl.BlockSpec(memory_space=pl.ANY), vmem, vmem, vmem, vmem],
        out_specs=vmem,
        scratch_shapes=[
            pltpu.VMEM((rows, width), bf16),
            pltpu.VMEM((96, BLK, BLK), bf16),
            pltpu.VMEM((96, BLK, BLK), bf16),
            pltpu.VMEM((BLK, BLK), bf16),
            pltpu.VMEM((rows, BLK), f32),
            pltpu.VMEM((rows, NH * BLK), bf16),
            pltpu.VMEM((HALF, BLK, BLK), f32),
            pltpu.VMEM((HALF, BLK, BLK), bf16),
            pltpu.VMEM((HALF, BLK, BLK), bf16),
            dma, dma, dma((96,)), dma, dma((96,)), dma, dma, dma((NH,)), dma((NH,)), dma((HALF,)), dma((HALF,)),
        ],
        compiler_params=pltpu.CompilerParams(collective_id=0, has_side_effects=True, vmem_limit_bytes=48 << 20),
        cost_estimate=pl.CostEstimate(flops=805306368, bytes_accessed=4 << 20, transcendentals=0),
    )(decode_states, query_weight, query_exponents, output_weight, output_exponents)


def solution(mesh):
    return jax.shard_map(
        per_device,
        mesh=mesh,
        in_specs=(
            P("dp", None),
            P("dp", "tensor"),
            P("dp", "tensor"),
            P("tensor", "dp"),
            P("tensor", "dp"),
        ),
        out_specs=P("dp", "tensor"),
        check_vma=False,
    )
```

```python
import functools

import jax
import jax.numpy as jnp
from jax import lax
from jax.experimental import pallas as pl
from jax.experimental.pallas import tpu as pltpu
from jax.sharding import PartitionSpec as P

MESH = pl.DeviceIdType.MESH
NX, NY, NZ, NH = 4, 8, 3, 4
BLK = 128
HALF = NZ * NY // 2
VMEM_LIMIT = 61 << 20


def device(x, y, zl, zh, c):
    return ((x * NZ + zl) * NY + y, zh * 2 + c)


def dense_block(weight_ref, exponent_ref):
    power = exponent_ref[...].astype(jnp.float32)
    inverse = jnp.exp2(-power).astype(jnp.bfloat16).astype(jnp.float32)
    scale = jnp.exp2(power).astype(jnp.bfloat16).astype(jnp.float32)
    codes = jnp.clip(weight_ref[...] * inverse, -448.0, 448.0).astype(jnp.bfloat16)
    return (codes.astype(jnp.float32) * scale).astype(jnp.bfloat16)


def kernel(x_hbm, qw_hbm, qe_ref, ow_hbm, oe_ref, out_ref,
           xv, qw_ref, ow_ref, wq, wqs, wo, wos, qacc, qown, qcat, pout, pin,
           x_sem, w_sems, own_send, wq_send, wq_recv, wo_send, wo_recv, a_send, b_send, q_send, q_recv, p_send, p_recv):
    d = lax.axis_index("dp")
    t = lax.axis_index("tensor")
    y = d % NY
    zl = (d // NY) % NZ
    x = d // (NY * NZ)
    zh = t // 2
    c = t % 2
    collector = x == zh

    def on(core, dx=0, dy=0, dz=0, dh=0):
        return device((x + dx) % NX, (y + dy) % NY, (zl + dz) % NZ, (zh + dh) % NH, core)

    def copy(src, dst, send, recv, to):
        return pltpu.make_async_remote_copy(src, dst, send, recv, device_id=to, device_id_type=MESH)

    qw_copy = pltpu.make_async_copy(qw_hbm, qw_ref, w_sems.at[0])
    ow_copy = pltpu.make_async_copy(ow_hbm, ow_ref, w_sems.at[1])
    x_copy = pltpu.make_async_copy(x_hbm, xv, x_sem)
    qw_copy.start()
    ow_copy.start()

    barrier = pltpu.get_barrier_semaphore()
    near = [dict(dx=1), dict(dx=3), dict(dy=1), dict(dy=7), dict(dz=1), dict(dz=2)]
    heads = [dict(dh=2), dict(dh=1), dict(dh=3)]

    def greet(core, where):
        pl.semaphore_signal(barrier, inc=1, device_id=on(core, **where), device_id_type=MESH)

    @pl.when(c == 0)
    def _():
        x_copy.start()
        for where in near:
            greet(0, where)
        for where in [{}] + near:
            greet(1, where)

    @pl.when(c == 1)
    def _():
        for where in heads:
            greet(1, where)
            greet(0, where)
        for where in [dict(dx=2)] + near:
            greet(1, where)
        greet(0, {})

    def qi(dx, dz, dy):
        return (((x + dx) % NX) * NZ + (zl + dz) % NZ) * NY + (y + dy) % NY

    def oi(dz, dy, h):
        return (((zl + dz) % NZ) * NY + (y + dy) % NY) * NH + h

    own_q = qi(0, 0, 0)
    own_o = oi(0, 0, zh)
    qw_copy.wait()
    wqs[...] = dense_block(qw_ref, qe_ref)
    ow_copy.wait()
    wos[...] = dense_block(ow_ref, oe_ref)

    def q_half(b):
        return wq.at[b, :, pl.ds(pl.multiple_of(c * BLK, BLK), BLK)]

    def o_half(b):
        return wo.at[b, pl.ds(pl.multiple_of(c * BLK, BLK), BLK)]

    def own_copy(to):
        return copy(wqs, q_half(own_q), own_send, wq_recv.at[own_q], to)

    def a_copy():
        return copy(wos, o_half(own_o), a_send, wo_recv.at[own_o], device(x, y, zl, x, 1))

    def q_copy(b, to):
        return copy(wq.at[b], wq.at[b], wq_send, wq_recv.at[b], to)

    def q_wait(b):
        q_copy(b, on(0, dx=1)).wait_recv()

    def o_copy(b, to, sem):
        return copy(wo.at[b], wo.at[b], sem, wo_recv.at[b], to)

    def o_wait(b):
        o_copy(b, on(1, dy=1), wo_send).wait_recv()

    def x_query(k):
        cols = qcat.at[:, pl.ds(pl.multiple_of(zh * 2 * BLK, 2 * BLK), 2 * BLK)]
        return copy(qown, cols, q_send.at[k], q_recv.at[zh], on(1, dh=k))

    def p_copy(j, core):
        return copy(pout.at[j], pin.at[j], p_send.at[j], p_recv.at[j], on(core))

    def sent(ref, sem):
        copy(ref, ref, sem, wo_recv.at[0], on(1 - c)).wait_send()

    def query_core():
        half = q_half(own_q)
        half[...] = wqs[...]
        pl.semaphore_wait(barrier, 10)
        a_copy().start()
        for where in (dict(dz=1), dict(dz=2), dict(dy=1), dict(dy=7), dict(dx=1), dict(dx=3)):
            own_copy(on(0, **where)).start()

        def planes(b):
            q_copy(b, on(0, dx=1)).start()
            q_copy(b, on(0, dx=3)).start()

        for dz in (1, 2):
            b = qi(0, dz, 0)
            q_wait(b)
            q_copy(b, on(0, dy=1)).start()
            q_copy(b, on(0, dy=7)).start()
            planes(b)

        @pl.loop(0, 9)
        def _(n):
            k = 1 + n // NZ
            dz = n % NZ
            left, right = qi(0, dz, NY - k), qi(0, dz, k)
            even = ((zl + dz) % NZ + y + k) % 2 == 0
            q_wait(left)

            @pl.when(jnp.logical_or(k < 3, even))
            def _():
                q_copy(left, on(0, dy=1)).start()

            planes(left)
            q_wait(right)

            @pl.when(jnp.logical_or(k < 3, jnp.logical_not(even)))
            def _():
                q_copy(right, on(0, dy=7)).start()

            planes(right)

        @pl.loop(0, NZ)
        def _(dz):
            b = qi(0, dz, 4)
            q_wait(b)
            planes(b)

        own = q_half(own_q)
        copy(own, own, wq_send, wq_recv.at[own_q], on(1)).wait_recv()
        x_copy.wait()
        qacc[...] = jnp.zeros_like(qacc)

        def q_dot(dx, dz):
            chunk = ((x + dx) % NX) * NZ + (zl + dz) % NZ
            columns = pl.ds(pl.multiple_of(chunk * (NY * BLK), NY * BLK), NY * BLK)
            w = wq[pl.ds(chunk * NY, NY)].reshape(NY * BLK, 2 * BLK)
            qacc[...] += jnp.dot(xv[:, columns], w, preferred_element_type=jnp.float32)

        @pl.loop(0, NZ * NY)
        def _(m):
            r = jnp.maximum(m - NZ, 0)
            k = jnp.where(m < NZ, 0, 1 + r // 6)
            dz = jnp.where(m < NZ, m, jnp.where(r < 18, (r % 6) // 2, r - 18))
            dy = jnp.where(r % 2 == 0, NY - k, k)
            even = ((y + dy) % NY) % 2 == 0
            left = qi(3, dz, dy)
            right = qi(1, dz, dy)
            q_wait(left)

            @pl.when(even)
            def _():
                q_copy(left, on(0, dx=1)).start()

            q_wait(right)

            @pl.when(jnp.logical_not(even))
            def _():
                q_copy(right, on(0, dx=3)).start()

            @pl.when(m % 8 == 4)
            def _():
                q_dot(0, m // 8)

        @pl.loop(0, 6)
        def _(m):
            q_dot(3 - 2 * (m % 2), m // 2)

        @pl.loop(0, NZ)
        def _(dz):
            @pl.loop(0, NY)
            def _(n):
                q_wait(qi(2, dz, n))

            q_dot(2, dz)

        qown[...] = qacc[...].astype(jnp.bfloat16)
        for k in (2, 1, 3, 0):
            x_query(k).start()

        for j in range(HALF):
            p_copy(j, 1).wait_recv()
            out_ref[:, j * BLK:(j + 1) * BLK] = pin[j]

        for k in range(NH):
            x_query(k).wait_send()
        sent(wq.at[pl.ds(0, 89)], wq_send)
        sent(pin.at[pl.ds(0, 6)], own_send)
        sent(wos, a_send)

    def output_core():
        @pl.when(collector)
        def _():
            half = o_half(own_o)
            half[...] = wos[...]

        pl.semaphore_wait(barrier, 17)

        @pl.when(jnp.logical_not(collector))
        def _():
            a_copy().start()

        for where in (dict(dz=1), dict(dz=2), dict(dy=1), dict(dy=7), dict(dx=1), dict(dx=3), {}):
            own_copy(on(0, **where)).start()

        def group(i):
            return (zh + jnp.where(i == 2, 3, jnp.where(i == 3, 2, i))) % NH

        def spread(b):
            o_copy(b, on(1, dy=1), wo_send).start()
            o_copy(b, on(1, dy=7), wo_send).start()

        def lanes(b):
            o_copy(b, on(1, dz=1), wo_send).start()
            o_copy(b, on(1, dz=2), wo_send).start()

        @pl.loop(0, NH)
        def _(i):
            b = oi(0, 0, group(i))
            mine = jnp.logical_and(collector, i == 0)

            @pl.when(mine)
            def _():
                other = wo.at[own_o, pl.ds(0, BLK)]
                copy(other, other, wo_send, wo_recv.at[own_o], on(0)).wait_recv()

            @pl.when(jnp.logical_not(mine))
            def _():
                o_wait(b)

            @pl.when(collector)
            def _():
                for k in (2, 1, 3):
                    o_copy(b, on(1, dx=k), b_send).start()

            spread(b)
            lanes(b)

        @pl.loop(0, NH - 1)
        def _(i):
            for dz in (1, 2):
                b = oi(dz, 0, group(i))
                o_wait(b)
                spread(b)

        def ring(r, k):
            i = jnp.where(r == 0, NH - 1, lax.rem(r + 2, 3))
            dz = jnp.where(r == 0, 0, (r - 1) // 3)
            h = group(i)
            even = ((zl + dz) % NZ + h + (y + k)) % 2 == 0
            return oi(dz, NY - k, h), oi(dz, k, h), even

        @pl.loop(0, 30)
        def _(m):
            r = m % 10
            k = 1 + m // 10
            left, right, even = ring(r, k)
            o_wait(left)

            @pl.when(jnp.logical_or(k < 3, even))
            def _():
                o_copy(left, on(1, dy=1), wo_send).start()

            o_wait(right)

            @pl.when(jnp.logical_or(k < 3, jnp.logical_not(even)))
            def _():
                o_copy(right, on(1, dy=7), wo_send).start()

            @pl.when(r == 0)
            def _():
                lanes(left)
                lanes(right)

        @pl.loop(0, 10)
        def _(r):
            last, _, _ = ring(r, 4)
            o_wait(last)

            @pl.when(r == 0)
            def _():
                lanes(last)

        @pl.loop(0, NY)
        def _(n):
            for dz in (1, 2):
                o_wait(oi(dz, n, group(NH - 1)))

        for k in range(NH):
            h = (zh + k) % NH
            cols = qcat.at[:, pl.ds(pl.multiple_of(h * 2 * BLK, 2 * BLK), 2 * BLK)]
            copy(cols, cols, q_send.at[k], q_recv.at[h], on(0, dh=k)).wait_recv()

        def whole_sum(j):
            w = wo[pl.ds(j * NH, NH)].reshape(NH * 2 * BLK, BLK)
            return jnp.dot(qcat[...], w, preferred_element_type=jnp.float32).astype(jnp.bfloat16)

        @pl.loop(0, HALF)
        def _(j):
            pout[j] = whole_sum(j)
            p_copy(j, 0).start()

        for j in range(HALF):
            out_ref[:, j * BLK:(j + 1) * BLK] = whole_sum(HALF + j)

        for j in range(HALF):
            p_copy(j, 0).wait_send()
        sent(wo.at[pl.ds(0, 92)], wo_send)
        sent(pin.at[pl.ds(0, 7)], own_send)

        @pl.when(collector)
        def _():
            sent(wo.at[pl.ds(0, 12)], b_send)

        @pl.when(jnp.logical_not(collector))
        def _():
            sent(wos, a_send)

    pl.when(c == 0)(query_core)
    pl.when(c == 1)(output_core)


def per_device(decode_states, query_weight, query_exponents, output_weight, output_exponents):
    rows, width = decode_states.shape
    vmem = pl.BlockSpec(memory_space=pltpu.VMEM)
    hbm = pl.BlockSpec(memory_space=pltpu.HBM)
    bf16, f32 = jnp.bfloat16, jnp.float32
    dma = pltpu.SemaphoreType.DMA
    return pl.pallas_call(
        kernel,
        out_shape=jax.ShapeDtypeStruct((rows, HALF * BLK), bf16),
        in_specs=[hbm, hbm, vmem, hbm, vmem],
        out_specs=vmem,
        scratch_shapes=[
            pltpu.VMEM((rows, width), bf16),
            pltpu.VMEM((BLK, BLK), f32),
            pltpu.VMEM((BLK, BLK), f32),
            pltpu.VMEM((96, BLK, 2 * BLK), bf16),
            pltpu.VMEM((BLK, BLK), bf16),
            pltpu.VMEM((96, 2 * BLK, BLK), bf16),
            pltpu.VMEM((BLK, BLK), bf16),
            pltpu.VMEM((rows, 2 * BLK), f32),
            pltpu.VMEM((rows, 2 * BLK), bf16),
            pltpu.VMEM((rows, 2 * NH * BLK), bf16),
            pltpu.VMEM((HALF, BLK, BLK), bf16),
            pltpu.VMEM((HALF, BLK, BLK), bf16),
            dma, dma((2,)), dma, dma, dma((96,)), dma, dma((96,)), dma, dma, dma((NH,)), dma((NH,)), dma((HALF,)), dma((HALF,)),
        ],
        compiler_params=pltpu.CompilerParams(collective_id=0, has_side_effects=True, vmem_limit_bytes=VMEM_LIMIT),
        cost_estimate=pl.CostEstimate(flops=805306368, bytes_accessed=4 << 20, transcendentals=0),
    )(decode_states, query_weight, query_exponents, output_weight, output_exponents)


def solution(mesh):
    return jax.shard_map(
        per_device,
        mesh=mesh,
        in_specs=(
            P("dp", None),
            P("dp", "tensor"),
            P("dp", "tensor"),
            P("tensor", "dp"),
            P("tensor", "dp"),
        ),
        out_specs=P("dp", "tensor"),
        check_vma=False,
    )
```

```python
import functools

import jax
import jax.numpy as jnp
from jax import lax
from jax.experimental import pallas as pl
from jax.experimental.pallas import tpu as pltpu
from jax.sharding import PartitionSpec as P

MESH = pl.DeviceIdType.MESH
NX, NY, NZ, NH = 4, 8, 3, 4
BLK = 128
HALF = NZ * NY // 2
VMEM_LIMIT = 61 << 20


def device(x, y, zl, zh, c):
    return ((x * NZ + zl) * NY + y, zh * 2 + c)


def dense_block(weight_ref, exponent_ref):
    power = exponent_ref[...].astype(jnp.float32)
    inverse = jnp.exp2(-power).astype(jnp.bfloat16).astype(jnp.float32)
    scale = jnp.exp2(power).astype(jnp.bfloat16).astype(jnp.float32)
    codes = jnp.clip(weight_ref[...] * inverse, -448.0, 448.0).astype(jnp.bfloat16)
    return (codes.astype(jnp.float32) * scale).astype(jnp.bfloat16)


def kernel(x_hbm, qw_hbm, qe_ref, ow_hbm, oe_ref, out_ref,
           xv, qw_ref, ow_ref, wq, wqs, wo, wos, qacc, qown, qcat, pout, pin,
           x_sem, w_sems, own_send, wq_send, wq_recv, wo_send, wo_recv, a_send, b_send, q_send, q_recv, p_send, p_recv):
    d = lax.axis_index("dp")
    t = lax.axis_index("tensor")
    y = d % NY
    zl = (d // NY) % NZ
    x = d // (NY * NZ)
    zh = t // 2
    c = t % 2
    collector = x == zh
    behind = (x + NX - zh) % NX

    def on(core, dx=0, dy=0, dz=0, dh=0):
        return device((x + dx) % NX, (y + dy) % NY, (zl + dz) % NZ, (zh + dh) % NH, core)

    def copy(src, dst, send, recv, to):
        return pltpu.make_async_remote_copy(src, dst, send, recv, device_id=to, device_id_type=MESH)

    qw_copy = pltpu.make_async_copy(qw_hbm, qw_ref, w_sems.at[0])
    ow_copy = pltpu.make_async_copy(ow_hbm, ow_ref, w_sems.at[1])
    x_copy = pltpu.make_async_copy(x_hbm, xv, x_sem)
    qw_copy.start()
    ow_copy.start()

    barrier = pltpu.get_barrier_semaphore()
    near = [dict(dx=1), dict(dx=3), dict(dy=1), dict(dy=7), dict(dz=1), dict(dz=2)]
    heads = [dict(dh=2), dict(dh=1), dict(dh=3)]

    def greet(core, where):
        pl.semaphore_signal(barrier, inc=1, device_id=on(core, **where), device_id_type=MESH)

    @pl.when(c == 0)
    def _():
        x_copy.start()
        for where in near:
            greet(0, where)
        for where in [{}] + near:
            greet(1, where)

    @pl.when(c == 1)
    def _():
        for where in heads:
            greet(1, where)
            greet(0, where)
        for where in near:
            greet(1, where)
        greet(0, {})

    def qi(dx, dz, dy):
        return (((x + dx) % NX) * NZ + (zl + dz) % NZ) * NY + (y + dy) % NY

    def oi(dz, dy, h):
        return (((zl + dz) % NZ) * NY + (y + dy) % NY) * NH + h

    own_q = qi(0, 0, 0)
    own_o = oi(0, 0, zh)
    qw_copy.wait()
    wqs[...] = dense_block(qw_ref, qe_ref)
    ow_copy.wait()
    wos[...] = dense_block(ow_ref, oe_ref)

    def q_half(b):
        return wq.at[b, :, pl.ds(pl.multiple_of(c * BLK, BLK), BLK)]

    def o_half(b):
        return wo.at[b, pl.ds(pl.multiple_of(c * BLK, BLK), BLK)]

    def own_copy(to):
        return copy(wqs, q_half(own_q), own_send, wq_recv.at[own_q], to)

    def a_copy():
        return copy(wos, o_half(own_o), a_send, wo_recv.at[own_o], device(x, y, zl, x, 1))

    def q_copy(b, to):
        return copy(wq.at[b], wq.at[b], wq_send, wq_recv.at[b], to)

    def q_wait(b):
        q_copy(b, on(0, dx=1)).wait_recv()

    def o_copy(b, to, sem):
        return copy(wo.at[b], wo.at[b], sem, wo_recv.at[b], to)

    def o_wait(b):
        o_copy(b, on(1, dy=1), wo_send).wait_recv()

    def x_query(k):
        cols = qcat.at[:, pl.ds(pl.multiple_of(zh * 2 * BLK, 2 * BLK), 2 * BLK)]
        return copy(qown, cols, q_send.at[k], q_recv.at[zh], on(1, dh=k))

    def p_copy(j, core):
        return copy(pout.at[j], pin.at[j], p_send.at[j], p_recv.at[j], on(core))

    def sent(ref, sem):
        copy(ref, ref, sem, wo_recv.at[0], on(1 - c)).wait_send()

    def query_core():
        half = q_half(own_q)
        half[...] = wqs[...]
        pl.semaphore_wait(barrier, 10)
        a_copy().start()
        for where in (dict(dz=1), dict(dz=2), dict(dy=1), dict(dy=7), dict(dx=1), dict(dx=3)):
            own_copy(on(0, **where)).start()

        def planes(b):
            q_copy(b, on(0, dx=1)).start()
            q_copy(b, on(0, dx=3)).start()

        for dz in (1, 2):
            b = qi(0, dz, 0)
            q_wait(b)
            q_copy(b, on(0, dy=1)).start()
            q_copy(b, on(0, dy=7)).start()
            planes(b)

        def crossing(left, right, even):
            q_wait(left)

            @pl.when(even)
            def _():
                q_copy(left, on(0, dx=1)).start()

            q_wait(right)

            @pl.when(jnp.logical_not(even))
            def _():
                q_copy(right, on(0, dx=3)).start()

        def opposite(dy):
            crossing(qi(3, 0, dy), qi(1, 0, dy), (zl + y + dy) % 2 == 0)

        def lanes(dy):
            b = qi(2, 0, dy)
            q_wait(b)
            q_copy(b, on(0, dz=1)).start()
            q_copy(b, on(0, dz=2)).start()

        @pl.loop(0, 9)
        def _(n):
            k = 1 + n // NZ
            dz = n % NZ
            left, right = qi(0, dz, NY - k), qi(0, dz, k)
            even = ((zl + dz) % NZ + y + k) % 2 == 0
            q_wait(left)

            @pl.when(jnp.logical_or(k < 3, even))
            def _():
                q_copy(left, on(0, dy=1)).start()

            planes(left)
            q_wait(right)

            @pl.when(jnp.logical_or(k < 3, jnp.logical_not(even)))
            def _():
                q_copy(right, on(0, dy=7)).start()

            planes(right)

            @pl.when(n == 2)
            def _():
                opposite(0)

            @pl.when(n == 5)
            def _():
                opposite(1)
                opposite(7)
                lanes(0)

            @pl.when(n == 8)
            def _():
                lanes(1)
                lanes(7)

        @pl.loop(0, NZ)
        def _(dz):
            b = qi(0, dz, 4)
            q_wait(b)
            planes(b)

        own = q_half(own_q)
        copy(own, own, wq_send, wq_recv.at[own_q], on(1)).wait_recv()
        x_copy.wait()
        qacc[...] = jnp.zeros_like(qacc)

        def place(m):
            r = jnp.maximum(m - NZ, 0)
            k = jnp.where(m < NZ, 0, 1 + r // 6)
            dz = jnp.where(m < NZ, m, jnp.where(r < 18, (r % 6) // 2, r - 18))
            return dz, jnp.where(r % 2 == 0, NY - k, k)

        def q_dot(*blocks):
            lhs = [xv[:, pl.ds(pl.multiple_of(b * BLK, BLK), BLK)] for b in blocks]
            rhs = [wq[b] for b in blocks]
            qacc[...] += jnp.dot(
                jnp.concatenate(lhs, axis=1), jnp.concatenate(rhs, axis=0), preferred_element_type=jnp.float32)

        @pl.loop(0, NZ * NY)
        def _(m):
            dz, dy = place(m)
            left = qi(3, dz, dy)
            right = qi(1, dz, dy)

            @pl.when(m >= 9)
            def _():
                crossing(left, right, ((zl + dz) % NZ + (y + dy) % NY) % 2 == 0)

            @pl.when(jnp.logical_and(m < 9, dz > 0))
            def _():
                q_wait(left)
                q_wait(right)

            q_dot(qi(0, dz, dy), left, right)

        @pl.loop(0, NZ * NY // 2)
        def _(n):
            pair = []
            for m in (2 * n, 2 * n + 1):
                dz, dy = place(m)
                b = qi(2, dz, dy)
                pl.when(jnp.logical_or(m >= 9, dz > 0))(functools.partial(q_wait, b))
                pair.append(b)
            q_dot(*pair)

        qown[...] = qacc[...].astype(jnp.bfloat16)
        for k in (2, 1, 3, 0):
            x_query(k).start()

        for j in range(HALF):
            p_copy(j, 1).wait_recv()
            out_ref[:, j * BLK:(j + 1) * BLK] = pin[j]

        for k in range(NH):
            x_query(k).wait_send()
        sent(wq.at[pl.ds(0, 89)], wq_send)
        sent(pin.at[pl.ds(0, 6)], own_send)
        sent(wos, a_send)

    def output_core():
        @pl.when(collector)
        def _():
            half = o_half(own_o)
            half[...] = wos[...]

        pl.semaphore_wait(barrier, 16)

        @pl.when(jnp.logical_not(collector))
        def _():
            a_copy().start()

        for where in (dict(dz=1), dict(dz=2), dict(dy=1), dict(dy=7), dict(dx=1), dict(dx=3), {}):
            own_copy(on(0, **where)).start()

        def group(i):
            return (zh + jnp.where(i == 2, 3, jnp.where(i == 3, 2, i))) % NH

        def spread(b):
            o_copy(b, on(1, dy=1), wo_send).start()
            o_copy(b, on(1, dy=7), wo_send).start()

        def lanes(b):
            o_copy(b, on(1, dz=1), wo_send).start()
            o_copy(b, on(1, dz=2), wo_send).start()

        @pl.loop(0, NH)
        def _(i):
            b = oi(0, 0, group(i))
            mine = jnp.logical_and(collector, i == 0)

            @pl.when(mine)
            def _():
                other = wo.at[own_o, pl.ds(0, BLK)]
                copy(other, other, wo_send, wo_recv.at[own_o], on(0)).wait_recv()

            @pl.when(jnp.logical_not(mine))
            def _():
                o_wait(b)

            @pl.when(collector)
            def _():
                for k in (1, 3):
                    o_copy(b, on(1, dx=k), b_send).start()

            @pl.when(jnp.logical_and(behind == 1, i % 2 == 0))
            def _():
                o_copy(b, on(1, dx=1), b_send).start()

            @pl.when(jnp.logical_and(behind == 3, i % 2 == 1))
            def _():
                o_copy(b, on(1, dx=3), b_send).start()

            spread(b)
            lanes(b)

        @pl.loop(0, NH - 1)
        def _(i):
            for dz in (1, 2):
                b = oi(dz, 0, group(i))
                o_wait(b)
                spread(b)

        def ring(r, k):
            i = jnp.where(r == 0, NH - 1, lax.rem(r + 2, 3))
            dz = jnp.where(r == 0, 0, (r - 1) // 3)
            h = group(i)
            even = ((zl + dz) % NZ + h + (y + k)) % 2 == 0
            return oi(dz, NY - k, h), oi(dz, k, h), even

        @pl.loop(0, 30)
        def _(m):
            r = m % 10
            k = 1 + m // 10
            left, right, even = ring(r, k)
            o_wait(left)

            @pl.when(jnp.logical_or(k < 3, even))
            def _():
                o_copy(left, on(1, dy=1), wo_send).start()

            o_wait(right)

            @pl.when(jnp.logical_or(k < 3, jnp.logical_not(even)))
            def _():
                o_copy(right, on(1, dy=7), wo_send).start()

            @pl.when(r == 0)
            def _():
                lanes(left)
                lanes(right)

        @pl.loop(0, 10)
        def _(r):
            last, _, _ = ring(r, 4)
            o_wait(last)

            @pl.when(r == 0)
            def _():
                lanes(last)

        @pl.loop(0, NY)
        def _(n):
            for dz in (1, 2):
                o_wait(oi(dz, n, group(NH - 1)))

        for k in range(NH):
            h = (zh + k) % NH
            cols = qcat.at[:, pl.ds(pl.multiple_of(h * 2 * BLK, 2 * BLK), 2 * BLK)]
            copy(cols, cols, q_send.at[k], q_recv.at[h], on(0, dh=k)).wait_recv()

        def pair_sum(j):
            w = [wo[pl.ds((j + k) * NH, NH)].reshape(NH * 2 * BLK, BLK) for k in (0, 1)]
            return jnp.dot(qcat[...], jnp.concatenate(w, axis=1), preferred_element_type=jnp.float32).astype(jnp.bfloat16)

        @pl.loop(0, HALF // 2)
        def _(n):
            j = 2 * n
            both = pair_sum(j)
            pout[j] = both[:, :BLK]
            pout[j + 1] = both[:, BLK:]
            p_copy(j, 0).start()
            p_copy(j + 1, 0).start()

        for j in range(0, HALF, 2):
            out_ref[:, j * BLK:(j + 2) * BLK] = pair_sum(HALF + j)

        for j in range(HALF):
            p_copy(j, 0).wait_send()
        sent(wo.at[pl.ds(0, 92)], wo_send)
        sent(pin.at[pl.ds(0, 7)], own_send)

        @pl.when(collector)
        def _():
            sent(wo.at[pl.ds(0, 8)], b_send)

        @pl.when(behind % 2 == 1)
        def _():
            sent(wo.at[pl.ds(0, 2)], b_send)

        @pl.when(jnp.logical_not(collector))
        def _():
            sent(wos, a_send)

    pl.when(c == 0)(query_core)
    pl.when(c == 1)(output_core)


def per_device(decode_states, query_weight, query_exponents, output_weight, output_exponents):
    rows, width = decode_states.shape
    vmem = pl.BlockSpec(memory_space=pltpu.VMEM)
    hbm = pl.BlockSpec(memory_space=pltpu.HBM)
    bf16, f32 = jnp.bfloat16, jnp.float32
    dma = pltpu.SemaphoreType.DMA
    return pl.pallas_call(
        kernel,
        out_shape=jax.ShapeDtypeStruct((rows, HALF * BLK), bf16),
        in_specs=[hbm, hbm, vmem, hbm, vmem],
        out_specs=vmem,
        scratch_shapes=[
            pltpu.VMEM((rows, width), bf16),
            pltpu.VMEM((BLK, BLK), f32),
            pltpu.VMEM((BLK, BLK), f32),
            pltpu.VMEM((96, BLK, 2 * BLK), bf16),
            pltpu.VMEM((BLK, BLK), bf16),
            pltpu.VMEM((96, 2 * BLK, BLK), bf16),
            pltpu.VMEM((BLK, BLK), bf16),
            pltpu.VMEM((rows, 2 * BLK), f32),
            pltpu.VMEM((rows, 2 * BLK), bf16),
            pltpu.VMEM((rows, 2 * NH * BLK), bf16),
            pltpu.VMEM((HALF, BLK, BLK), bf16),
            pltpu.VMEM((HALF, BLK, BLK), bf16),
            dma, dma((2,)), dma, dma, dma((96,)), dma, dma((96,)), dma, dma, dma((NH,)), dma((NH,)), dma((HALF,)), dma((HALF,)),
        ],
        compiler_params=pltpu.CompilerParams(collective_id=0, has_side_effects=True, vmem_limit_bytes=VMEM_LIMIT),
        cost_estimate=pl.CostEstimate(flops=805306368, bytes_accessed=4 << 20, transcendentals=0),
    )(decode_states, query_weight, query_exponents, output_weight, output_exponents)


def solution(mesh):
    return jax.shard_map(
        per_device,
        mesh=mesh,
        in_specs=(
            P("dp", None),
            P("dp", "tensor"),
            P("dp", "tensor"),
            P("tensor", "dp"),
            P("tensor", "dp"),
        ),
        out_specs=P("dp", "tensor"),
        check_vma=False,
    )
```

```python
import functools

import jax
import jax.numpy as jnp
from jax import lax
from jax.experimental import pallas as pl
from jax.experimental.pallas import tpu as pltpu
from jax.sharding import PartitionSpec as P

MESH = pl.DeviceIdType.MESH
NX, NY, NZ, NH = 4, 8, 3, 4
BLK = 128
HALF = NZ * NY // 2
AHEAD = 7
VMEM_LIMIT = 61 << 20


def device(x, y, zl, zh, c):
    return ((x * NZ + zl) * NY + y, zh * 2 + c)


def dense_block(weight_ref, exponent_ref):
    power = exponent_ref[...].astype(jnp.float32)
    inverse = jnp.exp2(-power).astype(jnp.bfloat16).astype(jnp.float32)
    scale = jnp.exp2(power).astype(jnp.bfloat16).astype(jnp.float32)
    codes = jnp.clip(weight_ref[...] * inverse, -448.0, 448.0).astype(jnp.bfloat16)
    return (codes.astype(jnp.float32) * scale).astype(jnp.bfloat16)


def kernel(x_hbm, qw_hbm, qe_ref, ow_hbm, oe_ref, out_ref,
           xv, qw_ref, ow_ref, wq, wqs, wo, wos, qacc, qown, qcat, pout, pin,
           x_sem, w_sems, own_send, wq_send, wq_recv, wo_send, wo_recv, a_send, b_send, q_send, q_recv, p_send, p_recv):
    d = lax.axis_index("dp")
    t = lax.axis_index("tensor")
    y = d % NY
    zl = (d // NY) % NZ
    x = d // (NY * NZ)
    zh = t // 2
    c = t % 2
    collector = x == zh
    behind = (x + NX - zh) % NX

    def on(core, dx=0, dy=0, dz=0, dh=0):
        return device((x + dx) % NX, (y + dy) % NY, (zl + dz) % NZ, (zh + dh) % NH, core)

    def copy(src, dst, send, recv, to):
        return pltpu.make_async_remote_copy(src, dst, send, recv, device_id=to, device_id_type=MESH)

    qw_copy = pltpu.make_async_copy(qw_hbm, qw_ref, w_sems.at[0])
    ow_copy = pltpu.make_async_copy(ow_hbm, ow_ref, w_sems.at[1])
    x_copy = pltpu.make_async_copy(x_hbm, xv, x_sem)
    qw_copy.start()
    ow_copy.start()

    barrier = pltpu.get_barrier_semaphore()
    near = [dict(dx=1), dict(dx=3), dict(dy=1), dict(dy=7), dict(dz=1), dict(dz=2)]
    heads = [dict(dh=2), dict(dh=1), dict(dh=3)]

    def greet(core, where):
        pl.semaphore_signal(barrier, inc=1, device_id=on(core, **where), device_id_type=MESH)

    @pl.when(c == 0)
    def _():
        x_copy.start()
        for where in near:
            greet(0, where)
        for where in [{}] + near:
            greet(1, where)

    @pl.when(c == 1)
    def _():
        for where in heads:
            greet(1, where)
            greet(0, where)
        for where in near:
            greet(1, where)
        greet(0, {})

    def qi(dx, dz, dy):
        return (((x + dx) % NX) * NZ + (zl + dz) % NZ) * NY + (y + dy) % NY

    def oi(dz, dy, h):
        return (((zl + dz) % NZ) * NY + (y + dy) % NY) * NH + h

    own_q = qi(0, 0, 0)
    own_o = oi(0, 0, zh)
    qw_copy.wait()
    wqs[...] = dense_block(qw_ref, qe_ref)
    ow_copy.wait()
    wos[...] = dense_block(ow_ref, oe_ref)

    def q_half(b):
        return wq.at[b, :, pl.ds(pl.multiple_of(c * BLK, BLK), BLK)]

    def o_half(b):
        return wo.at[b, pl.ds(pl.multiple_of(c * BLK, BLK), BLK)]

    def own_copy(to):
        return copy(wqs, q_half(own_q), own_send, wq_recv.at[own_q], to)

    def a_copy():
        return copy(wos, o_half(own_o), a_send, wo_recv.at[own_o], device(x, y, zl, x, 1))

    def q_copy(b, to):
        return copy(wq.at[b], wq.at[b], wq_send, wq_recv.at[b], to)

    def q_wait(b):
        q_copy(b, on(0, dx=1)).wait_recv()

    def o_copy(b, to, sem):
        return copy(wo.at[b], wo.at[b], sem, wo_recv.at[b], to)

    def o_wait(b):
        o_copy(b, on(1, dy=1), wo_send).wait_recv()

    def x_query(k):
        cols = qcat.at[:, pl.ds(pl.multiple_of(zh * 2 * BLK, 2 * BLK), 2 * BLK)]
        return copy(qown, cols, q_send.at[k], q_recv.at[zh], on(1, dh=k))

    def p_copy(j, core):
        return copy(pout.at[j], pin.at[j], p_send.at[j], p_recv.at[j], on(core))

    def sent(ref, sem):
        copy(ref, ref, sem, wo_recv.at[0], on(1 - c)).wait_send()

    def query_core():
        half = q_half(own_q)
        half[...] = wqs[...]
        pl.semaphore_wait(barrier, 10)
        a_copy().start()
        for where in (dict(dz=1), dict(dz=2), dict(dy=1), dict(dy=7), dict(dx=1), dict(dx=3)):
            own_copy(on(0, **where)).start()

        def planes(b):
            q_copy(b, on(0, dx=1)).start()
            q_copy(b, on(0, dx=3)).start()

        for dz in (1, 2):
            b = qi(0, dz, 0)
            q_wait(b)
            q_copy(b, on(0, dy=1)).start()
            q_copy(b, on(0, dy=7)).start()
            planes(b)

        def crossing(left, right, even):
            q_wait(left)

            @pl.when(even)
            def _():
                q_copy(left, on(0, dx=1)).start()

            q_wait(right)

            @pl.when(jnp.logical_not(even))
            def _():
                q_copy(right, on(0, dx=3)).start()

        def opposite(dy):
            crossing(qi(3, 0, dy), qi(1, 0, dy), (zl + y + dy) % 2 == 0)

        def lanes(dy):
            b = qi(2, 0, dy)
            q_wait(b)
            q_copy(b, on(0, dz=1)).start()
            q_copy(b, on(0, dz=2)).start()

        @pl.loop(0, 9)
        def _(n):
            k = 1 + n // NZ
            dz = n % NZ
            left, right = qi(0, dz, NY - k), qi(0, dz, k)
            even = ((zl + dz) % NZ + y + k) % 2 == 0
            q_wait(left)

            @pl.when(jnp.logical_or(k < 3, even))
            def _():
                q_copy(left, on(0, dy=1)).start()

            planes(left)
            q_wait(right)

            @pl.when(jnp.logical_or(k < 3, jnp.logical_not(even)))
            def _():
                q_copy(right, on(0, dy=7)).start()

            planes(right)

            @pl.when(n == 2)
            def _():
                opposite(0)

            @pl.when(n == 5)
            def _():
                opposite(1)
                opposite(7)
                lanes(0)


        @pl.loop(0, NZ)
        def _(dz):
            b = qi(0, dz, 4)
            q_wait(b)
            planes(b)

        lanes(1)
        lanes(7)

        own = q_half(own_q)
        copy(own, own, wq_send, wq_recv.at[own_q], on(1)).wait_recv()
        x_copy.wait()
        qacc[...] = jnp.zeros_like(qacc)

        def place(m):
            r = jnp.maximum(m - NZ, 0)
            k = jnp.where(m < NZ, 0, 1 + r // 6)
            dz = jnp.where(m < NZ, m, jnp.where(r < 18, (r % 6) // 2, r - 18))
            return dz, jnp.where(r % 2 == 0, NY - k, k)

        def q_dot(*blocks):
            lhs = [xv[:, pl.ds(pl.multiple_of(b * BLK, BLK), BLK)] for b in blocks]
            rhs = [wq[b] for b in blocks]
            qacc[...] += jnp.dot(
                jnp.concatenate(lhs, axis=1), jnp.concatenate(rhs, axis=0), preferred_element_type=jnp.float32)

        @pl.loop(0, NZ * NY)
        def _(m):
            dz, dy = place(m)
            left = qi(3, dz, dy)
            right = qi(1, dz, dy)

            @pl.when(m >= 9)
            def _():
                crossing(left, right, ((zl + dz) % NZ + (y + dy) % NY) % 2 == 0)

            @pl.when(jnp.logical_and(m < 9, dz > 0))
            def _():
                q_wait(left)
                q_wait(right)

            q_dot(qi(0, dz, dy), left, right)

        @pl.loop(0, NZ * NY // 2)
        def _(n):
            pair = []
            for m in (2 * n, 2 * n + 1):
                dz, dy = place(m)
                b = qi(2, dz, dy)
                pl.when(jnp.logical_or(m >= 9, dz > 0))(functools.partial(q_wait, b))
                pair.append(b)
            q_dot(*pair)

        qown[...] = qacc[...].astype(jnp.bfloat16)
        for k in (2, 1, 3, 0):
            x_query(k).start()

        for j in range(HALF):
            p_copy(j, 1).wait_recv()
            out_ref[:, j * BLK:(j + 1) * BLK] = pin[j]

        for k in range(NH):
            x_query(k).wait_send()
        sent(wq.at[pl.ds(0, 89)], wq_send)
        sent(pin.at[pl.ds(0, 6)], own_send)
        sent(wos, a_send)

    def output_core():
        @pl.when(collector)
        def _():
            half = o_half(own_o)
            half[...] = wos[...]

        pl.semaphore_wait(barrier, 16)

        @pl.when(jnp.logical_not(collector))
        def _():
            a_copy().start()

        for where in (dict(dz=1), dict(dz=2), dict(dy=1), dict(dy=7), dict(dx=1), dict(dx=3), {}):
            own_copy(on(0, **where)).start()

        def group(i):
            return (zh + jnp.where(i == 2, 3, jnp.where(i == 3, 2, i))) % NH

        def spread(b):
            o_copy(b, on(1, dy=1), wo_send).start()
            o_copy(b, on(1, dy=7), wo_send).start()

        def lanes(b):
            o_copy(b, on(1, dz=1), wo_send).start()
            o_copy(b, on(1, dz=2), wo_send).start()

        @pl.loop(0, NH)
        def _(i):
            b = oi(0, 0, group(i))
            mine = jnp.logical_and(collector, i == 0)

            @pl.when(mine)
            def _():
                other = wo.at[own_o, pl.ds(0, BLK)]
                copy(other, other, wo_send, wo_recv.at[own_o], on(0)).wait_recv()

            @pl.when(jnp.logical_not(mine))
            def _():
                o_wait(b)

            @pl.when(collector)
            def _():
                for k in (1, 3):
                    o_copy(b, on(1, dx=k), b_send).start()

            @pl.when(jnp.logical_and(behind == 1, i % 2 == 0))
            def _():
                o_copy(b, on(1, dx=1), b_send).start()

            @pl.when(jnp.logical_and(behind == 3, i % 2 == 1))
            def _():
                o_copy(b, on(1, dx=3), b_send).start()

            spread(b)
            lanes(b)

        @pl.loop(0, NH - 1)
        def _(i):
            for dz in (1, 2):
                b = oi(dz, 0, group(i))
                o_wait(b)
                spread(b)

        def ring(r, k):
            i = jnp.where(r == 0, NH - 1, lax.rem(r + 2, 3))
            dz = jnp.where(r == 0, 0, (r - 1) // 3)
            h = group(i)
            even = ((zl + dz) % NZ + h + (y + k)) % 2 == 0
            return oi(dz, NY - k, h), oi(dz, k, h), even

        def hop(r, k):
            left, right, even = ring(r, k)
            o_wait(left)

            @pl.when(jnp.logical_or(k < 3, even))
            def _():
                o_copy(left, on(1, dy=1), wo_send).start()

            o_wait(right)

            @pl.when(jnp.logical_or(k < 3, jnp.logical_not(even)))
            def _():
                o_copy(right, on(1, dy=7), wo_send).start()

            return left, right

        @pl.loop(0, 27)
        def _(m):
            @pl.when(jnp.logical_and(m % AHEAD == 0, m < 3 * AHEAD))
            def _():
                left, right = hop(0, 1 + m // AHEAD)
                lanes(left)
                lanes(right)

            @pl.when(m == 3 * AHEAD)
            def _():
                last, _, _ = ring(0, 4)
                o_wait(last)
                lanes(last)

            hop(1 + m % 9, 1 + m // 9)

        @pl.loop(1, 10)
        def _(r):
            last, _, _ = ring(r, 4)
            o_wait(last)

        @pl.loop(0, NY)
        def _(n):
            for dz in (1, 2):
                o_wait(oi(dz, n, group(NH - 1)))

        for k in range(NH):
            h = (zh + k) % NH
            cols = qcat.at[:, pl.ds(pl.multiple_of(h * 2 * BLK, 2 * BLK), 2 * BLK)]
            copy(cols, cols, q_send.at[k], q_recv.at[h], on(0, dh=k)).wait_recv()

        def pair_sum(j):
            w = [wo[pl.ds((j + k) * NH, NH)].reshape(NH * 2 * BLK, BLK) for k in (0, 1)]
            return jnp.dot(qcat[...], jnp.concatenate(w, axis=1), preferred_element_type=jnp.float32).astype(jnp.bfloat16)

        @pl.loop(0, HALF // 2)
        def _(n):
            j = 2 * n
            both = pair_sum(j)
            pout[j] = both[:, :BLK]
            pout[j + 1] = both[:, BLK:]
            p_copy(j, 0).start()
            p_copy(j + 1, 0).start()

        for j in range(0, HALF, 2):
            out_ref[:, j * BLK:(j + 2) * BLK] = pair_sum(HALF + j)

        for j in range(HALF):
            p_copy(j, 0).wait_send()
        sent(wo.at[pl.ds(0, 92)], wo_send)
        sent(pin.at[pl.ds(0, 7)], own_send)

        @pl.when(collector)
        def _():
            sent(wo.at[pl.ds(0, 8)], b_send)

        @pl.when(behind % 2 == 1)
        def _():
            sent(wo.at[pl.ds(0, 2)], b_send)

        @pl.when(jnp.logical_not(collector))
        def _():
            sent(wos, a_send)

    pl.when(c == 0)(query_core)
    pl.when(c == 1)(output_core)


def per_device(decode_states, query_weight, query_exponents, output_weight, output_exponents):
    rows, width = decode_states.shape
    vmem = pl.BlockSpec(memory_space=pltpu.VMEM)
    hbm = pl.BlockSpec(memory_space=pltpu.HBM)
    bf16, f32 = jnp.bfloat16, jnp.float32
    dma = pltpu.SemaphoreType.DMA
    return pl.pallas_call(
        kernel,
        out_shape=jax.ShapeDtypeStruct((rows, HALF * BLK), bf16),
        in_specs=[hbm, hbm, vmem, hbm, vmem],
        out_specs=vmem,
        scratch_shapes=[
            pltpu.VMEM((rows, width), bf16),
            pltpu.VMEM((BLK, BLK), f32),
            pltpu.VMEM((BLK, BLK), f32),
            pltpu.VMEM((96, BLK, 2 * BLK), bf16),
            pltpu.VMEM((BLK, BLK), bf16),
            pltpu.VMEM((96, 2 * BLK, BLK), bf16),
            pltpu.VMEM((BLK, BLK), bf16),
            pltpu.VMEM((rows, 2 * BLK), f32),
            pltpu.VMEM((rows, 2 * BLK), bf16),
            pltpu.VMEM((rows, 2 * NH * BLK), bf16),
            pltpu.VMEM((HALF, BLK, BLK), bf16),
            pltpu.VMEM((HALF, BLK, BLK), bf16),
            dma, dma((2,)), dma, dma, dma((96,)), dma, dma((96,)), dma, dma, dma((NH,)), dma((NH,)), dma((HALF,)), dma((HALF,)),
        ],
        compiler_params=pltpu.CompilerParams(collective_id=0, has_side_effects=True, vmem_limit_bytes=VMEM_LIMIT),
        cost_estimate=pl.CostEstimate(flops=805306368, bytes_accessed=4 << 20, transcendentals=0),
    )(decode_states, query_weight, query_exponents, output_weight, output_exponents)


def solution(mesh):
    return jax.shard_map(
        per_device,
        mesh=mesh,
        in_specs=(
            P("dp", None),
            P("dp", "tensor"),
            P("dp", "tensor"),
            P("tensor", "dp"),
            P("tensor", "dp"),
        ),
        out_specs=P("dp", "tensor"),
        check_vma=False,
    )
```
